256 devices in a mesh: row: 32 (over y, x, core), col: 8 (over z).
Axes of the slice: x: 4, y: 4, z: 8, core: 2. Of those that a mesh axis runs over, the one named last changes fastest.
Arguments:
- start: float32 [65536, 128], P(('row', 'col')), may hold values from -6 to 6
- tiles: float32 [256, 24, 256, 256], P(('row', 'col')), may hold values from -0.375 to 0.375
- tile_rows: int32 [256, 24], P(('row', 'col')), may hold values from 0 to 7, as said below
- tile_cols: int32 [256, 24], P(('row', 'col')), may hold values from 0 to 31, as said below
- tile_count: int32 [256], P(('row', 'col')), may hold values from 1 to 24, as said below
Outputs:
- basis: float32 [65536, 128], P(('row', 'col'))
- factor: float32 [128, 128], replicated
The draws below stay inside these ranges and needn't reach their ends.
Inputs may be any that keep to these rules, and one draw needn't show every extreme that they name: Within the first tile_count[d] slots of a device the pairs (tile_rows, tile_cols) are distinct; later slots may hold anything in range. `tile_cols`: see tile_rows. `tile_count`: counts differ from device to device; some device is full.
All inputs are finite; a program needn't handle non-finite values.
Results may differ from the reference program's by a relative error of at most 0.0003.
Values sent between devices are 32-bit elements; how exact they have to be, the bound alone decides.
A program may use at most 64 MiB of HBM per device.

```python
import jax
import jax.numpy as jnp
from jax import lax

TILE = 256
VEC = 128
ITERS = 2
K_DEV = 24
NODES = 65536
N_ROW = 32
N_COL = 8
DEVICES = 256


def layout(key):
    device = jnp.arange(DEVICES, dtype=jnp.int32)
    slots = jnp.arange(N_COL * N_ROW, dtype=jnp.int32)
    local_a = slots // N_ROW
    local_b = slots % N_ROW
    keys = jax.random.split(jax.random.fold_in(key, 11), DEVICES)
    shuffled = jax.vmap(lambda one: jax.random.permutation(one, N_COL * N_ROW))(keys).astype(jnp.int32)
    forced = (device[:, None] == N_COL) & (slots[None, :] == 0)
    score = jnp.where(forced, -1, shuffled)
    order = jnp.argsort(score, axis=1, stable=True)[:, :K_DEV]
    rows = local_a[order].astype(jnp.int32)
    cols = local_b[order].astype(jnp.int32)
    drawn = jax.random.randint(jax.random.fold_in(key, 12), (DEVICES,), K_DEV // 4, K_DEV + 1).astype(jnp.int32)
    count = jnp.maximum(drawn, 1)
    count = jnp.where(device == N_COL - 1, K_DEV, count).astype(jnp.int32)
    return (rows, cols, count)


def draw_tile_rows(key, part):
    return layout(key)[0]


def draw_tile_cols(key, part):
    return layout(key)[1]


def draw_tile_count(key, part):
    return layout(key)[2]


def block_scale(own_key, dims, cuts, smallest, top_value):
    gain, own = 1.0, jax.random.fold_in(own_key, 6)
    for axis_at, blocks in cuts:
        heights = jnp.exp(jax.random.uniform(jax.random.fold_in(own, axis_at), (blocks,), jnp.float32, smallest / len(cuts), top_value / len(cuts)))
        gain = gain * jnp.repeat(heights, dims[axis_at] // blocks).reshape([-1 if axis == axis_at else 1 for axis in range(len(dims))])
    return gain


def scatter_about(key, extent, scale, reach, cuts=(), kind=jnp.bfloat16):
    gain = block_scale(key, extent, cuts, -0.22, 0.18) if cuts else 1.0
    values = jax.random.normal(key, extent, jnp.float32) * scale * gain
    return jnp.minimum(jnp.maximum(values, -reach), reach).astype(kind)


def setup_inputs(seed: int = 0) -> dict:
    streams_of = jax.random.split(jax.random.key(seed), 6)
    return {
        "start": scatter_about(streams_of[0], (NODES, VEC), 1.0, 6.0, ((0, 256),), jnp.float32),
        "tiles": scatter_about(streams_of[1], (DEVICES, K_DEV, TILE, TILE), TILE ** -0.5, 0.375, ((0, 256),), jnp.float32),
        "tile_rows": draw_tile_rows(jax.random.fold_in(streams_of[5], 71), 0),
        "tile_cols": draw_tile_cols(jax.random.fold_in(streams_of[5], 71), 0),
        "tile_count": draw_tile_count(jax.random.fold_in(streams_of[5], 71), 0),
    }


def multiply(vectors, tiles, tile_rows, tile_cols, tile_count):
    blocks = vectors.reshape(DEVICES, TILE, VEC)
    slot_ids = jnp.arange(K_DEV, dtype=jnp.int32)

    def visit(total, device):
        first = device // N_COL * N_COL + tile_rows[device]
        second = tile_cols[device] * N_COL + device % N_COL
        live = (slot_ids < tile_count[device]).astype(jnp.float32)[:, None, None]
        pieces = tiles[device].astype(jnp.float32)
        upper = jnp.einsum('kpq,kqf->kpf', pieces, blocks[second], precision=lax.Precision.HIGHEST)
        mirror = jnp.einsum('kqp,kqf->kpf', pieces, blocks[first], precision=lax.Precision.HIGHEST)
        total = total.at[first].add(upper * live)
        total = total.at[second].add(mirror * live)
        return (total, None)
    result, unused = lax.scan(visit, jnp.zeros((DEVICES, TILE, VEC), jnp.float32), jnp.arange(DEVICES, dtype=jnp.int32))
    return result.reshape(NODES, VEC)

def reference(start, tiles, tile_rows, tile_cols, tile_count):
    basis = start
    factor = jnp.zeros((VEC, VEC), jnp.float32)
    for step in range(ITERS):
        image = multiply(basis, tiles, tile_rows, tile_cols, tile_count)
        gram = jnp.dot(image.T.astype(jnp.float32), image.astype(jnp.float32), precision=lax.Precision.HIGHEST, preferred_element_type=jnp.float32) / NODES
        factor = jnp.linalg.cholesky(gram)
        basis = jax.scipy.linalg.solve_triangular(factor, image.T, lower=True).T
    return (basis, factor)
```

```python
from types import SimpleNamespace

import jax
import jax.numpy as jnp
from jax import lax
from jax.experimental import pallas as pl
from jax.experimental.pallas import tpu as pltpu
from jax.sharding import PartitionSpec as P

ITERS = 2
VEC = 128
TILE = 256
SLOTS = 24
N_ROW = 32
N_COL = 8
SIDE = 4
HALF = VEC // 2
PART = VEC // N_COL
NODES = N_ROW * N_COL * TILE
MESH = pl.DeviceIdType.MESH
F32 = jnp.float32
BF16 = jnp.bfloat16
PANEL = 8

T_FAR, T_NEAR, T_PREV_FAR, T_PREV_NEAR, T_LAST_FAR, T_LAST_NEAR = 0, 24, 48, 72, 96, 128
T_SIZE = 136
MAX_COPIES = 170


def split(value):
    high = value.astype(BF16)
    return high, (value - high.astype(F32)).astype(BF16)


def exact(a, b, dims):
    return lax.dot_general(
        a, b, (dims, ((), ())), precision=lax.Precision.HIGHEST, preferred_element_type=F32
    )


def three_pass(x, high, low, contract):
    dims = (((1,), (contract,)), ((), ()))
    xh, xl = split(x)
    both = lax.dot_general(
        jnp.concatenate([xh, xl], axis=0), high, dims, preferred_element_type=F32
    )
    rest = lax.dot_general(xh, low, dims, preferred_element_type=F32)
    return both[:VEC] + (both[VEC:] + rest)


def comm_scratch():
    block = lambda *lead: pltpu.VMEM((*lead, VEC, TILE), F32)
    half = lambda *lead: pltpu.VMEM((*lead, HALF, TILE), F32)
    return dict(
        far=block(N_ROW),
        near=block(N_COL),
        pack=block(16),
        sib=block(16),
        total=block(16),
        ring2a=half(2, 4),
        ring2b=block(2, 4),
        col=block(4),
        ring1a=half(2),
        ring1b=block(2),
        nears=block(N_COL),
        zin=block(2, 4),
        gram=pltpu.VMEM((VEC, VEC), F32),
        gz=pltpu.VMEM((N_COL, PART, VEC), F32),
        gx=pltpu.VMEM((N_COL, PART, VEC), F32),
        gy=pltpu.VMEM((SIDE, PART, VEC), F32),
        gsum=pltpu.VMEM((VEC, VEC), F32),
    )


def own_scratch():
    return dict(
        tiles_in=pltpu.VMEM((SLOTS, TILE, TILE), F32),
        high=pltpu.VMEM((SLOTS, TILE, TILE), BF16),
        low=pltpu.VMEM((SLOTS, TILE, TILE), BF16),
        sum_far=pltpu.VMEM((SLOTS + 1, VEC, TILE), F32),
        sum_near=pltpu.VMEM((SLOTS + 1, VEC, TILE), F32),
        upper=pltpu.VMEM((VEC, VEC), F32),
        inverse=pltpu.VMEM((VEC, VEC), F32),
        tile_sem=pltpu.SemaphoreType.DMA,
        send=pltpu.SemaphoreType.DMA((ITERS, MAX_COPIES)),
        recv=pltpu.SemaphoreType.DMA((ITERS, MAX_COPIES)),
    )


class Net:
    def __init__(self, send, recv):
        self.send, self.recv, self.copies = send, recv, []

    def copy(self, src, dst, device):
        i = len(self.copies)
        one = pltpu.make_async_remote_copy(
            src_ref=src,
            dst_ref=dst,
            send_sem=self.send.at[i],
            recv_sem=self.recv.at[i],
            device_id=device,
            device_id_type=MESH,
        )
        one.start()
        self.copies.append(one)
        return one

    def drain(self):
        for one in self.copies:
            one.wait_send()


def place():
    r = lax.axis_index("row")
    z = lax.axis_index("col")
    s = r % 2
    x = (r // 2) % SIDE
    y = r // (2 * SIDE)
    p1 = x * (1 - s) + y * s
    p2 = y * (1 - s) + x * s
    step1 = 2 + 6 * s
    step2 = 8 - 6 * s

    def dev(q1, q2):
        return ((q1 % SIDE) * step1 + (q2 % SIDE) * step2 + s, z)

    def slot(q1, q2):
        return s * 16 + (q2 % SIDE) * SIDE + q1 % SIDE

    return SimpleNamespace(
        r=r, z=z, s=s, x=x, y=y, p1=p1, p2=p2, slot=slot,
        r1p=dev(p1 + 1, p2), r1m=dev(p1 + 3, p2),
        r2p=dev(p1, p2 + 1), r2m=dev(p1, p2 + 3),
        sib=(r + 1 - 2 * s, z),
        zp=(r, (z + 1) % N_COL), zm=(r, (z + N_COL - 1) % N_COL),
        z_peer=lambda d: (r, (z + d) % N_COL),
        x_peer=lambda dx, ds: (y * 8 + ((x + dx) % SIDE) * 2 + (s + ds) % 2, z),
        y_peer=lambda dy: (((y + dy) % SIDE) * 8 + x * 2 + s, z),
    )


X_OFFSETS = [(dx, ds) for dx in range(SIDE) for ds in range(2) if dx or ds]
LOW, HIGH = pl.ds(0, HALF), pl.ds(HALF, HALF)
HALVES = (LOW, HIGH)


def enter(me):
    barrier = pltpu.get_barrier_semaphore()
    peers = [me.z_peer(d) for d in range(1, N_COL)]
    peers += [me.x_peer(*o) for o in X_OFFSETS]
    peers += [me.y_peer(d) for d in range(1, SIDE)]
    for peer in peers:
        pl.semaphore_signal(barrier, inc=1, device_id=peer, device_id_type=MESH)
    pl.semaphore_wait(barrier, len(peers))


def gather(me, net, buf, event):
    far, near = buf.far, buf.near
    p1, p2, z, slot = me.p1, me.p2, me.z, me.slot
    sib = []

    def send(block, rows, device):
        ref = far.at[block] if rows is None else far.at[block, rows]
        return net.copy(ref, ref, device)

    def share(block):
        sib.append(send(block, None, me.sib))

    def z_send(block, half, device):
        ref = near.at[block % N_COL, HALVES[half]]
        return net.copy(ref, ref, device)

    own = slot(p1, p2)
    r1 = [send(own, None, me.r1p), send(own, None, me.r1m)]
    zs = {}
    for h in range(2):
        zs["p", 1, h] = z_send(z, h, me.zp)
        zs["m", 1, h] = z_send(z, h, me.zm)
    r2 = [(send(own, None, me.r2p), send(own, None, me.r2m))]
    share(own)
    event("start")

    def z_step(d, h):
        if not (d == 4 and h == 1):
            zs["p", d, h].wait_recv()
            if d < 3 or (d == 3 and h == 0):
                zs["p", d + 1, h] = z_send(z + N_COL - d, h, me.zp)
        if not (d == 4 and h == 0):
            zs["m", d, h].wait_recv()
            if d < 3 or (d == 3 and h == 1):
                zs["m", d + 1, h] = z_send(z + d, h, me.zm)

    def column(block):
        r2.append((send(block, None, me.r2p), send(block, None, me.r2m)))
        share(block)

    across = []

    def ring2(i, q1):
        up, down = r2[i]
        up.wait_recv()
        first = send(slot(q1, p2 + 3), LOW, me.r2p)
        share(slot(q1, p2 + 3))
        down.wait_recv()
        second = send(slot(q1, p2 + 1), HIGH, me.r2m)
        share(slot(q1, p2 + 1))
        across.append((first, second, slot(q1, p2 + 2)))

    z_step(1, 0)
    r1[0].wait_recv()
    left = slot(p1 + 3, p2)
    r1a = send(left, LOW, me.r1p)
    column(left)
    r1[1].wait_recv()
    right = slot(p1 + 1, p2)
    r1b = send(right, HIGH, me.r1m)
    column(right)
    z_step(1, 1)
    event("gather")
    ring2(0, p1)
    event("gather")
    r1a.wait_recv()
    r1b.wait_recv()
    column(slot(p1 + 2, p2))
    z_step(2, 0)
    event("gather")
    z_step(2, 1)
    ring2(1, p1 + 3)
    event("gather")
    z_step(3, 0)
    ring2(2, p1 + 1)
    event("gather")
    z_step(3, 1)
    ring2(3, p1 + 2)
    event("gather")
    for first, second, block in across:
        first.wait_recv()
        second.wait_recv()
        share(block)
        event("gather")
    z_step(4, 0)
    z_step(4, 1)
    event("gather")
    for one in sib:
        one.wait_recv()


def mirror_products(tab, own, buf):
    @pl.loop(0, SLOTS)
    def _(k):
        x = buf.near[tab[T_NEAR + k]]
        res = three_pass(x, own.high[k], own.low[k], 0)
        own.sum_far[k + 1] = res + own.sum_far[tab[T_PREV_FAR + k]]


def upper_products(tab, own, buf):
    @pl.loop(0, SLOTS)
    def _(k):
        x = buf.far[tab[T_FAR + k]]
        res = three_pass(x, own.high[k], own.low[k], 1)
        own.sum_near[k + 1] = res + own.sum_near[tab[T_PREV_NEAR + k]]


def reduce(me, net, tab, own, buf, event):
    p1, p2, z, s = me.p1, me.p2, me.z, me.s
    total, pack = buf.total, buf.pack

    mirror_products(tab, own, buf)
    sib = []
    for q2 in (p1 + 2, p1 + 1, p1 + 3, p1):
        base = (q2 % SIDE) * SIDE
        for q1 in range(SIDE):
            pack[base + q1] = own.sum_far[tab[T_LAST_FAR + (1 - s) * 16 + base + q1]]
        sib.append(
            net.copy(pack.at[pl.ds(base, SIDE)], buf.sib.at[pl.ds(base, SIDE)], me.sib)
        )
    upper_products(tab, own, buf)

    nears = buf.nears
    for a in range(N_COL):
        nears[a] = own.sum_near[tab[T_LAST_NEAR + a]]
    zs = {}

    def z_send(sign, d, h):
        block = (z + d) % N_COL if sign == "p" else (z + N_COL - d) % N_COL
        zs[sign, d, h] = net.copy(
            nears.at[block, HALVES[h]],
            buf.zin.at[0 if sign == "p" else 1, d - 1, HALVES[h]],
            me.zp if sign == "p" else me.zm,
        )

    def z_add(sign, d, h):
        zs[sign, d + 1, h].wait_recv()
        block = (z + d) % N_COL if sign == "p" else (z + N_COL - d) % N_COL
        nears[block, HALVES[h]] += buf.zin[0 if sign == "p" else 1, d, HALVES[h]]

    z_send("p", 4, 0)
    z_send("m", 4, 1)
    z_send("p", 3, 1)
    z_send("m", 3, 0)

    order1 = (p1 + 2, p1 + 1, p1 + 3, p1)

    def at(q1, q2):
        return (q2 % SIDE) * SIDE + q1 % SIDE

    def whole(i, q2):
        sib[i].wait_recv()
        for q1 in range(SIDE):
            b = at(q1, q2)
            total[b] = own.sum_far[tab[T_LAST_FAR + s * 16 + b]] + buf.sib[b]

    whole(0, p2 + 2)
    a_copies = []
    for i, q1 in enumerate(order1):
        b = at(q1, p2 + 2)
        a_copies.append(
            (
                net.copy(total.at[b, LOW], buf.ring2a.at[0, i], me.r2p),
                net.copy(total.at[b, HIGH], buf.ring2a.at[1, i], me.r2m),
            )
        )
    event("reduce")
    z_add("p", 3, 0)
    z_send("p", 3, 0)
    z_add("m", 3, 1)
    z_send("m", 3, 1)
    whole(1, p2 + 1)
    whole(2, p2 + 3)
    b_copies = []
    for i, q1 in enumerate(order1):
        a_copies[i][0].wait_recv()
        b = at(q1, p2 + 1)
        total[b, LOW] += buf.ring2a[0, i]
        up = net.copy(total.at[b], buf.ring2b.at[0, i], me.r2p)
        a_copies[i][1].wait_recv()
        b = at(q1, p2 + 3)
        total[b, HIGH] += buf.ring2a[1, i]
        down = net.copy(total.at[b], buf.ring2b.at[1, i], me.r2m)
        b_copies.append((up, down))
        if i == 1:
            z_add("p", 2, 1)
            z_send("p", 2, 1)
            z_add("m", 2, 0)
            z_send("m", 2, 0)
            event("reduce")
    z_add("p", 2, 0)
    z_send("p", 2, 0)
    z_add("m", 2, 1)
    z_send("m", 2, 1)
    whole(3, p2)
    event("reduce")

    col = buf.col

    def gathered(i, q1):
        for one in b_copies[i]:
            one.wait_recv()
        col[i] = total[at(q1, p2)] + (buf.ring2b[0, i] + buf.ring2b[1, i])

    gathered(0, order1[0])
    a1 = net.copy(col.at[0, LOW], buf.ring1a.at[0], me.r1p)
    a2 = net.copy(col.at[0, HIGH], buf.ring1a.at[1], me.r1m)
    z_add("p", 1, 1)
    z_send("p", 1, 1)
    z_add("m", 1, 0)
    z_send("m", 1, 0)
    event("reduce")
    gathered(1, order1[1])
    a1.wait_recv()
    col[1, LOW] += buf.ring1a[0]
    b1 = net.copy(col.at[1], buf.ring1b.at[0], me.r1p)
    event("reduce")
    gathered(2, order1[2])
    a2.wait_recv()
    col[2, HIGH] += buf.ring1a[1]
    b2 = net.copy(col.at[2], buf.ring1b.at[1], me.r1m)
    z_add("p", 1, 0)
    z_send("p", 1, 0)
    z_add("m", 1, 1)
    z_send("m", 1, 1)
    event("reduce")
    gathered(3, order1[3])
    for sign in "pm":
        for h in range(2):
            z_add(sign, 0, h)
            if sign == "p" and h == 1:
                event("reduce")
    b1.wait_recv()
    b2.wait_recv()
    return (col[3] + nears[z]) + (buf.ring1b[0] + buf.ring1b[1])


def gram_steps(me, net, own, buf, image):
    buf.gram[...] = exact(image, image, ((1,), (1,))) * (1.0 / NODES)
    gz, gx, gy, gsum = buf.gz, buf.gx, buf.gy, buf.gsum

    def rows(c):
        return pl.ds(pl.multiple_of((c % N_COL) * PART, PART), PART)

    ones = [
        net.copy(buf.gram.at[rows(me.z + d)], gz.at[d], me.z_peer(d)) for d in range(1, N_COL)
    ]
    yield
    for one in ones:
        one.wait_recv()
    part = buf.gram[rows(me.z), :]
    for d in range(1, N_COL):
        part = part + gz[d]
    here = me.x * 2 + me.s
    gx[here] = part
    ones = [net.copy(gx.at[here], gx.at[here], me.x_peer(*o)) for o in X_OFFSETS]
    yield
    for one in ones:
        one.wait_recv()
    part = gx[0]
    for i in range(1, N_COL):
        part = part + gx[i]
    gy[me.y] = part
    ones = [net.copy(gy.at[me.y], gy.at[me.y], me.y_peer(d)) for d in range(1, SIDE)]
    yield
    for one in ones:
        one.wait_recv()
    part = gy[0]
    for i in range(1, SIDE):
        part = part + gy[i]
    gsum[rows(me.z), :] = part
    ones = [
        net.copy(gsum.at[rows(me.z)], gsum.at[rows(me.z)], me.z_peer(d))
        for d in range(1, N_COL)
    ]
    yield
    for one in ones:
        one.wait_recv()
    yield from cholesky_steps(own, gsum)


def cholesky_steps(own, gsum):
    upper, inverse = own.upper, own.inverse
    lane = lax.broadcasted_iota(jnp.int32, (VEC, VEC), 1)
    sub = lax.broadcasted_iota(jnp.int32, (VEC, VEC), 0)
    upper[...] = gsum[...]
    inverse[...] = jnp.where(lane == sub, 1.0, 0.0).astype(F32)
    for panel in range(0, VEC, PANEL):
        @pl.loop(panel, panel + PANEL)
        def _(j):
            row = upper[pl.ds(j, 1), :]
            row_inv = inverse[pl.ds(j, 1), :]
            pivot = jnp.sum(jnp.where(lane[:1] == j, row, 0.0), axis=1, keepdims=True)
            scale = 1.0 / jnp.sqrt(pivot)
            m = upper[...]
            below = (lane == j) & (sub > j)
            column = jnp.sum(jnp.where(below, m, 0.0), axis=1, keepdims=True) * scale
            u = row * scale
            v = row_inv * scale
            here = sub == j
            upper[...] = jnp.where(here, u, m - column * u)
            inverse[...] = jnp.where(here, v, inverse[...] - column * v)
        yield


def kernel(names, tab, start, tiles, basis, factor, *scratch):
    own_names, comm_names = names
    own = SimpleNamespace(**dict(zip(own_names, scratch)))
    rest = scratch[len(own_names):]
    bufs = [
        SimpleNamespace(**dict(zip(comm_names, rest[it * len(comm_names):])))
        for it in range(ITERS)
    ]
    me = place()
    loading = pltpu.make_async_copy(tiles, own.tiles_in, own.tile_sem)
    loading.start()
    image = start[...].T
    own.sum_far[0] = jnp.zeros((VEC, TILE), F32)
    own.sum_near[0] = jnp.zeros((VEC, TILE), F32)
    enter(me)

    for it in range(ITERS):
        buf = bufs[it]
        net = Net(own.send.at[it], own.recv.at[it])
        if it:
            steps = gram_steps(me, net, own, bufs[it - 1], image)
        buf.far[me.slot(me.p1, me.p2)] = image
        buf.near[me.z] = image

        def event(where):
            if it:
                next(steps, None)
            elif where == "start":
                loading.wait()

                @pl.loop(0, SLOTS)
                def _(k):
                    own.high[k], own.low[k] = split(own.tiles_in[k])

        gather(me, net, buf, event)
        image = reduce(me, net, tab, own, buf, event)
        if it:
            for _ in steps:
                pass
            image = exact(own.inverse[...], image, ((1,), (0,)))
            for _ in gram_steps(me, net, own, buf, image):
                pass
        net.drain()
    basis[...] = exact(own.inverse[...], image, ((1,), (0,))).T
    lane = lax.broadcasted_iota(jnp.int32, (VEC, VEC), 1)
    sub = lax.broadcasted_iota(jnp.int32, (VEC, VEC), 0)
    factor[...] = jnp.where(lane >= sub, own.upper[...], 0.0).T


def far_slot(b):
    s, x, y = b % 2, (b // 2) % SIDE, b // (2 * SIDE)
    return jnp.where(s == 0, y * SIDE + x, 16 + x * SIDE + y)


def table(rows, cols, count):
    slot = jnp.arange(SLOTS, dtype=jnp.int32)
    far = far_slot(cols)

    def latest(keys, blocks):
        asked = jnp.concatenate([keys, jnp.arange(blocks, dtype=jnp.int32)])
        before = jnp.concatenate([slot, jnp.full((blocks,), SLOTS, jnp.int32)])
        hit = (asked[:, None] == keys[None, :]) & (slot[None, :] < before[:, None])
        hit = hit & (slot[None, :] < count)
        return jnp.max(jnp.where(hit, slot[None, :] + 1, 0), axis=1)

    by_far = latest(far, N_ROW)
    by_near = latest(rows, N_COL)
    return jnp.concatenate(
        [far, rows, by_far[:SLOTS], by_near[:SLOTS], by_far[SLOTS:], by_near[SLOTS:]]
    )


def shards(start, tiles, tile_rows, tile_cols, tile_count):
    own, comm = own_scratch(), comm_scratch()
    names = (tuple(own), tuple(comm))
    vmem = pl.BlockSpec(memory_space=pltpu.VMEM)

    def body(*refs):
        kernel(names, *refs)

    return pl.pallas_call(
        body,
        out_shape=(
            jax.ShapeDtypeStruct((TILE, VEC), F32),
            jax.ShapeDtypeStruct((VEC, VEC), F32),
        ),
        in_specs=[
            pl.BlockSpec(memory_space=pltpu.SMEM),
            vmem,
            pl.BlockSpec(memory_space=pl.ANY),
        ],
        out_specs=(vmem, vmem),
        scratch_shapes=[*own.values(), *(ref for _ in range(ITERS) for ref in comm.values())],
        compiler_params=pltpu.CompilerParams(
            collective_id=0, has_side_effects=True, vmem_limit_bytes=62 * 1024 * 1024
        ),
    )(table(tile_rows[0], tile_cols[0], tile_count[0]), start, tiles[0])


def solution(mesh):
    placed = (
        P(("row", "col"), None),
        P(("row", "col"), None, None, None),
        P(("row", "col"), None),
        P(("row", "col"), None),
        P(("row", "col")),
    )
    return jax.shard_map(
        shards,
        mesh=mesh,
        in_specs=placed,
        out_specs=(P(("row", "col"), None), P()),
        check_vma=False,
    )
```

```python
from types import SimpleNamespace

import jax
import jax.numpy as jnp
from jax import lax
from jax.experimental import pallas as pl
from jax.experimental.pallas import tpu as pltpu
from jax.sharding import PartitionSpec as P

ITERS = 2
VEC = 128
TILE = 256
SLOTS = 24
N_ROW = 32
N_COL = 8
SIDE = 4
HALF = VEC // 2
PART = VEC // N_COL
NODES = N_ROW * N_COL * TILE
MESH = pl.DeviceIdType.MESH
F32 = jnp.float32
BF16 = jnp.bfloat16
PANEL = 32
GROUP = 16
UNROLL = 8
LAG = 0

T_PREV_FAR, T_PREV_NEAR, T_LAST_FAR, T_LAST_NEAR, T_FAR = 0, 24, 48, 80, 88
T_SIZE = 112
MAX_COPIES = 320


def split(value):
    high = value.astype(BF16)
    return high, (value - high.astype(F32)).astype(BF16)


def exact(a, b, dims):
    return lax.dot_general(
        a, b, (dims, ((), ())), precision=lax.Precision.HIGHEST, preferred_element_type=F32
    )


def three_pass(x, high, low, contract):
    dims = (((1,), (contract,)), ((), ()))
    xh, xl = split(x)
    both = lax.dot_general(
        jnp.concatenate([xh, xl], axis=0), high, dims, preferred_element_type=F32
    )
    rest = lax.dot_general(xh, low, dims, preferred_element_type=F32)
    return both[: x.shape[0]] + (both[x.shape[0] :] + rest)


def half_scratch():
    block = lambda *lead: pltpu.VMEM((*lead, HALF, TILE), F32)
    return dict(
        far=block(N_ROW),
        near=block(N_COL),
        pack=block(16),
        sib=block(16),
        total=block(16),
        ring2a=block(4),
        ring2b=block(2, 4),
        col=block(4),
        ring1a=block(1),
        ring1b=block(2),
        nears=block(N_COL),
        zin=block(2, 4),
    )


def gram_scratch():
    return dict(
        image=pltpu.VMEM((VEC, TILE), F32),
        gram=pltpu.VMEM((VEC, VEC), F32),
        gz=pltpu.VMEM((N_COL, PART, VEC), F32),
        gx=pltpu.VMEM((N_COL, PART, VEC), F32),
        gy=pltpu.VMEM((SIDE, PART, VEC), F32),
        gsum=pltpu.VMEM((VEC, VEC), F32),
    )


def own_scratch():
    sums = lambda: pltpu.VMEM((SLOTS + 1, HALF, TILE), F32)
    return dict(
        table=pltpu.SMEM((T_SIZE,), jnp.int32),
        tiles_in=pltpu.VMEM((SLOTS, TILE, TILE), F32),
        high=pltpu.VMEM((SLOTS, TILE, TILE), BF16),
        low=pltpu.VMEM((SLOTS, TILE, TILE), BF16),
        sum_far0=sums(),
        sum_far1=sums(),
        sum_near0=sums(),
        sum_near1=sums(),
        upper=pltpu.VMEM((VEC, VEC), F32),
        inverse=pltpu.VMEM((VEC, VEC), F32),
        tile_sem=pltpu.SemaphoreType.DMA,
        send=pltpu.SemaphoreType.DMA((MAX_COPIES,)),
        recv=pltpu.SemaphoreType.DMA((MAX_COPIES,)),
    )


class Net:
    def __init__(self, send, recv):
        self.send, self.recv, self.copies = send, recv, []

    def copy(self, src, dst, device):
        i = len(self.copies)
        one = pltpu.make_async_remote_copy(
            src_ref=src,
            dst_ref=dst,
            send_sem=self.send.at[i],
            recv_sem=self.recv.at[i],
            device_id=device,
            device_id_type=MESH,
        )
        one.start()
        self.copies.append(one)
        return one

    def drain(self):
        for one in self.copies:
            one.wait_send()


def place():
    r = lax.axis_index("row")
    z = lax.axis_index("col")
    s = r % 2
    x = (r // 2) % SIDE
    y = r // (2 * SIDE)
    p1 = x * (1 - s) + y * s
    p2 = y * (1 - s) + x * s
    step1 = 2 + 6 * s
    step2 = 8 - 6 * s

    def dev(q1, q2):
        return ((q1 % SIDE) * step1 + (q2 % SIDE) * step2 + s, z)

    def slot(q1, q2):
        return s * 16 + (q2 % SIDE) * SIDE + q1 % SIDE

    return SimpleNamespace(
        r=r, z=z, s=s, x=x, y=y, p1=p1, p2=p2, slot=slot,
        r1p=dev(p1 + 1, p2), r1m=dev(p1 + 3, p2),
        r2p=dev(p1, p2 + 1), r2m=dev(p1, p2 + 3),
        sib=(r + 1 - 2 * s, z),
        zp=(r, (z + 1) % N_COL), zm=(r, (z + N_COL - 1) % N_COL),
        z_peer=lambda d: (r, (z + d) % N_COL),
        x_peer=lambda dx, ds: (y * 8 + ((x + dx) % SIDE) * 2 + (s + ds) % 2, z),
        y_peer=lambda dy: (((y + dy) % SIDE) * 8 + x * 2 + s, z),
    )


X_OFFSETS = [(dx, ds) for dx in range(SIDE) for ds in range(2) if dx or ds]


def enter(me):
    barrier = pltpu.get_barrier_semaphore()
    peers = [me.z_peer(d) for d in range(1, N_COL)]
    peers += [me.x_peer(*o) for o in X_OFFSETS]
    peers += [me.y_peer(d) for d in range(1, SIDE)]
    for peer in peers:
        pl.semaphore_signal(barrier, inc=1, device_id=peer, device_id_type=MESH)
    pl.semaphore_wait(barrier, len(peers))


def gather_steps(h, me, net, buf):
    far, near = buf.far, buf.near
    p1, p2, z, slot = me.p1, me.p2, me.z, me.slot
    sib, r2, across = [], [], []
    zs = {}

    def send(block, device):
        return net.copy(far.at[block], far.at[block], device)

    def share(block):
        sib.append(send(block, me.sib))

    def z_send(block, device):
        ref = near.at[block % N_COL]
        return net.copy(ref, ref, device)

    def z_step(d):
        if d < 4 or h == 0:
            zs["p", d].wait_recv()
            if d < 3 or (d == 3 and h == 0):
                zs["p", d + 1] = z_send(z + N_COL - d, me.zp)
        if d < 4 or h == 1:
            zs["m", d].wait_recv()
            if d < 3 or (d == 3 and h == 1):
                zs["m", d + 1] = z_send(z + d, me.zm)

    def column(block):
        r2.append((send(block, me.r2p), send(block, me.r2m)))
        share(block)

    def ring2(i, q1):
        up, down = r2[i]
        up.wait_recv()
        if h == 0:
            on = send(slot(q1, p2 + 3), me.r2p)
        share(slot(q1, p2 + 3))
        down.wait_recv()
        if h == 1:
            on = send(slot(q1, p2 + 1), me.r2m)
        share(slot(q1, p2 + 1))
        across.append((on, slot(q1, p2 + 2)))

    own = slot(p1, p2)
    r1 = [send(own, me.r1p), send(own, me.r1m)]
    zs["p", 1] = z_send(z, me.zp)
    zs["m", 1] = z_send(z, me.zm)
    column(own)
    yield
    r1[0].wait_recv()
    if h == 0:
        on = send(slot(p1 + 3, p2), me.r1p)
    column(slot(p1 + 3, p2))
    r1[1].wait_recv()
    if h == 1:
        on = send(slot(p1 + 1, p2), me.r1m)
    column(slot(p1 + 1, p2))
    yield
    z_step(1)
    yield
    ring2(0, p1)
    yield
    on.wait_recv()
    column(slot(p1 + 2, p2))
    yield
    z_step(2)
    yield
    ring2(1, p1 + 3)
    yield
    ring2(2, p1 + 1)
    yield
    z_step(3)
    yield
    ring2(3, p1 + 2)
    yield
    for i, (one, block) in enumerate(across):
        one.wait_recv()
        share(block)
        if i % 2:
            yield
    z_step(4)
    yield
    for one in sib:
        one.wait_recv()


def mirror_products(rows, own, buf, sum_far):
    @pl.loop(0, SLOTS, unroll=UNROLL)
    def _(k):
        x = buf.near[rows[0, k]]
        res = three_pass(x, own.high[k], own.low[k], 0)
        sum_far[k + 1] = res + sum_far[own.table[T_PREV_FAR + k]]


def upper_products(own, buf, sum_near):
    @pl.loop(0, SLOTS, unroll=UNROLL)
    def _(k):
        x = buf.far[own.table[T_FAR + k]]
        res = three_pass(x, own.high[k], own.low[k], 1)
        sum_near[k + 1] = res + sum_near[own.table[T_PREV_NEAR + k]]


def reduce_steps(h, me, net, rows, own, buf, result):
    p1, p2, z, s = me.p1, me.p2, me.z, me.s
    total, pack, nears, tab = buf.total, buf.pack, buf.nears, own.table
    sum_far = (own.sum_far0, own.sum_far1)[h]
    sum_near = (own.sum_near0, own.sum_near1)[h]

    mirror_products(rows, own, buf, sum_far)
    sib = []
    for q2 in (p1 + 2, p1 + 1, p1 + 3, p1):
        base = (q2 % SIDE) * SIDE
        for q1 in range(SIDE):
            pack[base + q1] = sum_far[tab[T_LAST_FAR + (1 - s) * 16 + base + q1]]
        sib.append(
            net.copy(pack.at[pl.ds(base, SIDE)], buf.sib.at[pl.ds(base, SIDE)], me.sib)
        )
    yield
    upper_products(own, buf, sum_near)
    for a in range(N_COL):
        nears[a] = sum_near[tab[T_LAST_NEAR + a]]
    zs = {}
    order1 = (p1 + 2, p1 + 1, p1 + 3, p1)

    def z_block(sign, d):
        return (z + d) % N_COL if sign == "p" else (z + N_COL - d) % N_COL

    def z_send(sign, d):
        zs[sign, d] = net.copy(
            nears.at[z_block(sign, d)],
            buf.zin.at[0 if sign == "p" else 1, d - 1],
            me.zp if sign == "p" else me.zm,
        )

    def z_add(sign, d):
        if (sign, d + 1) in zs:
            zs[sign, d + 1].wait_recv()
            nears[z_block(sign, d)] += buf.zin[0 if sign == "p" else 1, d]

    def z_step(d):
        for sign in "pm":
            z_add(sign, d)
            z_send(sign, d)

    def at(q1, q2):
        return (q2 % SIDE) * SIDE + q1 % SIDE

    def whole(i, q2):
        sib[i].wait_recv()
        for q1 in range(SIDE):
            b = at(q1, q2)
            total[b] = sum_far[tab[T_LAST_FAR + s * 16 + b]] + buf.sib[b]

    z_send("pm"[h], 4)
    z_send("mp"[h], 3)
    whole(0, p2 + 2)
    ahead = [
        net.copy(total.at[at(q1, p2 + 2)], buf.ring2a.at[i], (me.r2p, me.r2m)[h])
        for i, q1 in enumerate(order1)
    ]
    plain, summed = ((p2 + 3, p2 + 1), (p2 + 1, p2 + 3))[h]
    whole((2, 1)[h], plain)
    plain_copies = [
        net.copy(total.at[at(q1, plain)], buf.ring2b.at[1 - h, i], (me.r2m, me.r2p)[h])
        for i, q1 in enumerate(order1)
    ]
    whole((1, 2)[h], summed)
    yield
    sign = "pm"[h]
    z_add(sign, 3)
    z_send(sign, 3)
    yield
    summed_copies = []
    for i, q1 in enumerate(order1):
        ahead[i].wait_recv()
        b = at(q1, summed)
        total[b] += buf.ring2a[i]
        summed_copies.append(net.copy(total.at[b], buf.ring2b.at[h, i], (me.r2p, me.r2m)[h]))
        if i == 1:
            yield
    whole(3, p2)
    yield
    z_step(2)
    yield
    col = buf.col

    def gathered(i):
        plain_copies[i].wait_recv()
        summed_copies[i].wait_recv()
        col[i] = total[at(order1[i], p2)] + (buf.ring2b[0, i] + buf.ring2b[1, i])

    gathered(0)
    on = net.copy(col.at[0], buf.ring1a.at[0], (me.r1p, me.r1m)[h])
    yield
    gathered(2 - h)
    b1 = net.copy(col.at[2 - h], buf.ring1b.at[1 - h], (me.r1m, me.r1p)[h])
    yield
    z_step(1)
    yield
    gathered(1 + h)
    on.wait_recv()
    col[1 + h] += buf.ring1a[0]
    b2 = net.copy(col.at[1 + h], buf.ring1b.at[h], (me.r1p, me.r1m)[h])
    gathered(3)
    yield
    z_add("p", 0)
    z_add("m", 0)
    part = col[3] + nears[z]
    yield
    b1.wait_recv()
    b2.wait_recv()
    part = part + (buf.ring1b[0] + buf.ring1b[1])
    result[HALF * h : HALF * (h + 1), :] = part


def pipe_steps(h, me, net, rows, own, bufs, grams, first):
    for it in range(ITERS):
        buf = bufs[it][h]
        image = first if it == 0 else grams[it - 1].image[HALF * h : HALF * (h + 1), :]
        buf.far[me.slot(me.p1, me.p2)] = image
        buf.near[me.z] = image
        yield from gather_steps(h, me, net, buf)
        yield
        yield from reduce_steps(h, me, net, rows, own, buf, grams[it].image)
        yield ("done", it)


def gram_steps(me, net, own, buf, image):
    buf.gram[...] = exact(image, image, ((1,), (1,))) * (1.0 / NODES)
    gz, gx, gy, gsum = buf.gz, buf.gx, buf.gy, buf.gsum

    def rows(c):
        return pl.ds(pl.multiple_of((c % N_COL) * PART, PART), PART)

    ones = [
        net.copy(buf.gram.at[rows(me.z + d)], gz.at[d], me.z_peer(d)) for d in range(1, N_COL)
    ]
    yield
    for one in ones:
        one.wait_recv()
    part = buf.gram[rows(me.z), :]
    for d in range(1, N_COL):
        part = part + gz[d]
    here = me.x * 2 + me.s
    gx[here] = part
    ones = [net.copy(gx.at[here], gx.at[here], me.x_peer(*o)) for o in X_OFFSETS]
    yield
    for one in ones:
        one.wait_recv()
    part = gx[0]
    for i in range(1, N_COL):
        part = part + gx[i]
    gy[me.y] = part
    ones = [net.copy(gy.at[me.y], gy.at[me.y], me.y_peer(d)) for d in range(1, SIDE)]
    yield
    for one in ones:
        one.wait_recv()
    part = gy[0]
    for i in range(1, SIDE):
        part = part + gy[i]
    gsum[rows(me.z), :] = part
    ones = [
        net.copy(gsum.at[rows(me.z)], gsum.at[rows(me.z)], me.z_peer(d))
        for d in range(1, N_COL)
    ]
    yield
    for one in ones:
        one.wait_recv()
    yield
    yield from cholesky_steps(own, gsum)


def cholesky_steps(own, gsum):
    upper, inverse = own.upper, own.inverse
    lane = lax.broadcasted_iota(jnp.int32, (VEC, VEC), 1)
    sub = lax.broadcasted_iota(jnp.int32, (VEC, VEC), 0)
    upper[...] = gsum[...]
    inverse[...] = jnp.where(lane == sub, 1.0, 0.0).astype(F32)
    strip = sub[:PANEL]
    for o in range(0, VEC, PANEL):
        p = upper[o : o + PANEL, :]
        a = inverse[o : o + PANEL, :]
        for first in range(0, PANEL, GROUP):
            columns = [
                jnp.broadcast_to(p[:, o + j : o + j + 1], (PANEL, VEC))
                for j in range(first, first + GROUP)
            ]
            for t in range(GROUP):
                j = first + t
                if j == PANEL - 1:
                    continue
                c = columns[t]
                m = jnp.where(strip > j, c, 0.0) * (1.0 / c[j : j + 1])
                for w in range(t + 1, GROUP):
                    columns[w] = columns[w] - m * c[first + w : first + w + 1]
                p, a = p - m * p[j : j + 1], a - m * a[j : j + 1]
        pivots = jnp.sum(jnp.where(lane[:PANEL] == strip + o, p, 0.0), axis=1, keepdims=True)
        scale = 1.0 / jnp.sqrt(pivots)
        p, a = p * scale, a * scale
        upper[o : o + PANEL, :] = p
        inverse[o : o + PANEL, :] = a
        if o + PANEL < VEC:
            below = p.T[o + PANEL :]
            upper[o + PANEL :, :] -= exact(below, p, ((1,), (0,)))
            inverse[o + PANEL :, :] -= exact(below, a, ((1,), (0,)))
        yield


def prepare_steps(rows, cols, count, own, loading):
    tab = own.table
    live = count[0]

    def latest(keys, key, before):
        found = jnp.int32(0)
        for k in range(SLOTS):
            hit = (keys[k] == key) & (k < before)
            found = jnp.where(hit, k + 1, found)
        return found

    cols_at = [cols[0, k] for k in range(SLOTS)]
    rows_at = [rows[0, k] for k in range(SLOTS)]

    @pl.loop(0, SLOTS)
    def _(k):
        b = cols[0, k]
        s, x, y = b % 2, (b // 2) % SIDE, b // (2 * SIDE)
        tab[T_FAR + k] = s * 16 + jnp.where(s == 0, y * SIDE + x, x * SIDE + y)
        tab[T_PREV_FAR + k] = latest(cols_at, b, jnp.minimum(k, live))
        tab[T_PREV_NEAR + k] = latest(rows_at, rows[0, k], jnp.minimum(k, live))

    yield

    @pl.loop(0, N_ROW)
    def _(i):
        s, q2, q1 = i // 16, (i // SIDE) % SIDE, i % SIDE
        x, y = q1 * (1 - s) + q2 * s, q2 * (1 - s) + q1 * s
        tab[T_LAST_FAR + i] = latest(cols_at, y * 8 + x * 2 + s, live)

    @pl.loop(0, N_COL)
    def _(i):
        tab[T_LAST_NEAR + i] = latest(rows_at, i, live)

    yield
    loading.wait()
    for first in range(0, SLOTS, 6):

        @pl.loop(first, first + 6)
        def _(k):
            own.high[k], own.low[k] = split(own.tiles_in[k])

        yield


def kernel(names, rows, cols, count, start, tiles, basis, factor, *scratch):
    own_names, gram_names, half_names = names
    refs = iter(scratch)
    take = lambda keys: SimpleNamespace(**{key: next(refs) for key in keys})
    own = take(own_names)
    grams = [take(gram_names) for _ in range(ITERS)]
    bufs = [[take(half_names) for _ in range(2)] for _ in range(ITERS)]
    me = place()
    loading = pltpu.make_async_copy(tiles, own.tiles_in, own.tile_sem)
    loading.start()
    image = start[...].T
    for ref in (own.sum_far0, own.sum_far1, own.sum_near0, own.sum_near1):
        ref[0] = jnp.zeros((HALF, TILE), F32)
    enter(me)

    net = Net(own.send, own.recv)
    pipes = [
        pipe_steps(h, me, net, rows, own, bufs, grams, image[HALF * h : HALF * (h + 1)])
        for h in range(2)
    ]
    beside = prepare_steps(rows, cols, count, own, loading)
    done = [None, None]
    tick = 0
    while any(d != ("done", ITERS - 1) for d in done):
        for h in range(2):
            if h == 0 or tick >= LAG:
                at = next(pipes[h], None)
                if at is not None:
                    done[h] = at
                    if at == ("done", 0) and done[1 - h] == ("done", 0):
                        beside = gram_steps(me, net, own, grams[0], grams[0].image[...])
        next(beside, None)
        tick += 1
    for _ in beside:
        pass
    image = exact(own.inverse[...], grams[1].image[...], ((1,), (0,)))
    for _ in gram_steps(me, net, own, grams[1], image):
        pass
    basis[...] = exact(own.inverse[...], image, ((1,), (0,))).T
    lane = lax.broadcasted_iota(jnp.int32, (VEC, VEC), 1)
    sub = lax.broadcasted_iota(jnp.int32, (VEC, VEC), 0)
    factor[...] = jnp.where(lane >= sub, own.upper[...], 0.0).T
    net.drain()


def shards(start, tiles, tile_rows, tile_cols, tile_count):
    own, gram, half = own_scratch(), gram_scratch(), half_scratch()
    names = (tuple(own), tuple(gram), tuple(half))
    vmem = pl.BlockSpec(memory_space=pltpu.VMEM)
    smem = pl.BlockSpec(memory_space=pltpu.SMEM)

    def body(*refs):
        kernel(names, *refs)

    return pl.pallas_call(
        body,
        out_shape=(
            jax.ShapeDtypeStruct((TILE, VEC), F32),
            jax.ShapeDtypeStruct((VEC, VEC), F32),
        ),
        in_specs=[smem, smem, smem, vmem, pl.BlockSpec(memory_space=pl.ANY)],
        out_specs=(vmem, vmem),
        scratch_shapes=[
            *own.values(),
            *(ref for _ in range(ITERS) for ref in gram.values()),
            *(ref for _ in range(2 * ITERS) for ref in half.values()),
        ],
        compiler_params=pltpu.CompilerParams(
            collective_id=0, has_side_effects=True, vmem_limit_bytes=62 * 1024 * 1024
        ),
    )(tile_rows, tile_cols, tile_count, start, tiles[0])


def solution(mesh):
    placed = (
        P(("row", "col"), None),
        P(("row", "col"), None, None, None),
        P(("row", "col"), None),
        P(("row", "col"), None),
        P(("row", "col")),
    )
    return jax.shard_map(
        shards,
        mesh=mesh,
        in_specs=placed,
        out_specs=(P(("row", "col"), None), P()),
        check_vma=False,
    )
```

```python
from types import SimpleNamespace

import jax
import jax.numpy as jnp
from jax import lax
from jax.experimental import pallas as pl
from jax.experimental.pallas import tpu as pltpu
from jax.sharding import PartitionSpec as P

ITERS = 2
VEC = 128
TILE = 256
SLOTS = 24
N_ROW = 32
N_COL = 8
SIDE = 4
PART = VEC // N_COL
NODES = N_ROW * N_COL * TILE
MESH = pl.DeviceIdType.MESH
F32 = jnp.float32
BF16 = jnp.bfloat16
PANEL = 32
GROUP = 16
UNROLL = 8
EVERY = 3
PIECES = 2

T_PREV_FAR, T_PREV_NEAR, T_LAST_FAR, T_LAST_NEAR, T_FAR = 0, 24, 48, 80, 88
T_SIZE = 112
MAX_COPIES = 320


def split(value):
    high = value.astype(BF16)
    return high, (value - high.astype(F32)).astype(BF16)


def exact(a, b, dims):
    return lax.dot_general(
        a, b, (dims, ((), ())), precision=lax.Precision.HIGHEST, preferred_element_type=F32
    )


def three_pass(x, high, low, contract):
    dims = (((1,), (contract,)), ((), ()))
    xh, xl = split(x)
    both = lax.dot_general(
        jnp.concatenate([xh, xl], axis=0), high, dims, preferred_element_type=F32
    )
    rest = lax.dot_general(xh, low, dims, preferred_element_type=F32)
    return both[: x.shape[0]] + (both[x.shape[0] :] + rest)


def block_scratch():
    block = lambda *lead: pltpu.VMEM((*lead, VEC, TILE), F32)
    return dict(
        far=block(N_ROW),
        near=block(N_COL),
        pack=block(16),
        sib=block(16),
        total=block(16),
        ring2a=block(4),
        ring2b=block(2, 4),
        col=block(4),
        ring1a=block(1),
        ring1b=block(2),
        nears=block(N_COL),
        zin=block(2, 4),
    )


def gram_scratch():
    return dict(
        image=pltpu.VMEM((VEC, TILE), F32),
        gram=pltpu.VMEM((VEC, VEC), F32),
        gz=pltpu.VMEM((N_COL, PART, VEC), F32),
        gx=pltpu.VMEM((N_COL, PART, VEC), F32),
        gy=pltpu.VMEM((SIDE, PART, VEC), F32),
        gsum=pltpu.VMEM((VEC, VEC), F32),
    )


def own_scratch():
    sums = lambda: pltpu.VMEM((SLOTS + 1, VEC, TILE), F32)
    return dict(
        table=pltpu.SMEM((T_SIZE,), jnp.int32),
        tiles_in=pltpu.VMEM((SLOTS, TILE, TILE), F32),
        high=pltpu.VMEM((SLOTS, TILE, TILE), BF16),
        low=pltpu.VMEM((SLOTS, TILE, TILE), BF16),
        sum_far=sums(),
        sum_near=sums(),
        upper=pltpu.VMEM((VEC, VEC), F32),
        inverse=pltpu.VMEM((VEC, VEC), F32),
        tile_sem=pltpu.SemaphoreType.DMA,
        send=pltpu.SemaphoreType.DMA((MAX_COPIES,)),
        recv=pltpu.SemaphoreType.DMA((MAX_COPIES,)),
    )


class Net:
    def __init__(self, send, recv):
        self.send, self.recv, self.copies = send, recv, []

    def copy(self, src, dst, device):
        i = len(self.copies)
        one = pltpu.make_async_remote_copy(
            src_ref=src,
            dst_ref=dst,
            send_sem=self.send.at[i],
            recv_sem=self.recv.at[i],
            device_id=device,
            device_id_type=MESH,
        )
        one.start()
        self.copies.append(one)
        return one

    def drain(self):
        for one in self.copies:
            one.wait_send()


def place():
    r = lax.axis_index("row")
    z = lax.axis_index("col")
    s = r % 2
    x = (r // 2) % SIDE
    y = r // (2 * SIDE)
    p1 = x * (1 - s) + y * s
    p2 = y * (1 - s) + x * s
    step1 = 2 + 6 * s
    step2 = 8 - 6 * s

    def dev(q1, q2):
        return ((q1 % SIDE) * step1 + (q2 % SIDE) * step2 + s, z)

    def slot(q1, q2):
        return s * 16 + (q2 % SIDE) * SIDE + q1 % SIDE

    return SimpleNamespace(
        r=r, z=z, s=s, x=x, y=y, p1=p1, p2=p2, slot=slot,
        r1p=dev(p1 + 1, p2), r1m=dev(p1 + 3, p2),
        r2p=dev(p1, p2 + 1), r2m=dev(p1, p2 + 3),
        r1far=dev(p1 + 2, p2), r2far=dev(p1, p2 + 2),
        sib=(r + 1 - 2 * s, z),
        zp=(r, (z + 1) % N_COL), zm=(r, (z + N_COL - 1) % N_COL),
        z_peer=lambda d: (r, (z + d) % N_COL),
        x_peer=lambda dx, ds: (y * 8 + ((x + dx) % SIDE) * 2 + (s + ds) % 2, z),
        y_peer=lambda dy: (((y + dy) % SIDE) * 8 + x * 2 + s, z),
    )


X_OFFSETS = [(dx, ds) for dx in range(SIDE) for ds in range(2) if dx or ds]


def enter(me):
    barrier = pltpu.get_barrier_semaphore()
    peers = [me.z_peer(d) for d in range(1, N_COL)]
    peers += [me.x_peer(*o) for o in X_OFFSETS]
    peers += [me.y_peer(d) for d in range(1, SIDE)]
    for peer in peers:
        pl.semaphore_signal(barrier, inc=1, device_id=peer, device_id_type=MESH)
    pl.semaphore_wait(barrier, len(peers))


def piece(j):
    return pl.ds(j * (VEC // PIECES), VEC // PIECES)


def gather_steps(me, net, buf, near_done):
    far, near = buf.far, buf.near
    p1, p2, z, slot = me.p1, me.p2, me.z, me.slot
    sib, r2, across = [], [], []
    zs = {}

    def send(block, device):
        return net.copy(far.at[block], far.at[block], device)

    def share(block):
        sib.append(send(block, me.sib))

    def z_send(block, j, device):
        ref = near.at[block % N_COL, piece(j)]
        return net.copy(ref, ref, device)

    def z_step(d):
        for j in range(PIECES):
            if d < 4 or j == 0:
                zs["p", d, j].wait_recv()
                if d < 3 or (d == 3 and j == 0):
                    zs["p", d + 1, j] = z_send(z + N_COL - d, j, me.zp)
            if d < 4 or j == 1:
                zs["m", d, j].wait_recv()
                if d < 3 or (d == 3 and j == 1):
                    zs["m", d + 1, j] = z_send(z + d, j, me.zm)

    def column(block):
        r2.append((send(block, me.r2p), send(block, me.r2m)))
        share(block)

    def ring2(i, q1):
        up, down = r2[i]
        on = far_column if i == 3 else None
        up.wait_recv()
        if i % 2 == 0 and on is None:
            on = send(slot(q1, p2 + 3), me.r2p)
        share(slot(q1, p2 + 3))
        down.wait_recv()
        if i % 2 == 1 and on is None:
            on = send(slot(q1, p2 + 1), me.r2m)
        share(slot(q1, p2 + 1))
        across.append((on, slot(q1, p2 + 2)))

    own = slot(p1, p2)
    r1 = [send(own, me.r1p), send(own, me.r1m)]
    for j in range(PIECES):
        zs["p", 1, j] = z_send(z, j, me.zp)
        zs["m", 1, j] = z_send(z, j, me.zm)
    column(own)
    on = send(own, me.r1far)
    yield
    r1[0].wait_recv()
    column(slot(p1 + 3, p2))
    r1[1].wait_recv()
    column(slot(p1 + 1, p2))
    yield
    z_step(1)
    yield
    ring2(0, p1)
    yield
    on.wait_recv()
    column(slot(p1 + 2, p2))
    far_column = send(slot(p1 + 2, p2), me.r2far)
    yield
    z_step(2)
    yield
    ring2(1, p1 + 3)
    yield
    ring2(2, p1 + 1)
    yield
    z_step(3)
    yield
    ring2(3, p1 + 2)
    yield
    z_step(4)
    near_done()
    yield
    for one, block in across:
        one.wait_recv()
        share(block)
    yield
    for one in sib:
        one.wait_recv()


def mirror_products(rows, own, buf, sum_far):
    @pl.loop(0, SLOTS, unroll=UNROLL)
    def _(k):
        x = buf.near[rows[0, k]]
        res = three_pass(x, own.high[k], own.low[k], 0)
        sum_far[k + 1] = res + sum_far[own.table[T_PREV_FAR + k]]


def upper_products(own, buf, sum_near):
    @pl.loop(0, SLOTS, unroll=UNROLL)
    def _(k):
        x = buf.far[own.table[T_FAR + k]]
        res = three_pass(x, own.high[k], own.low[k], 1)
        sum_near[k + 1] = res + sum_near[own.table[T_PREV_NEAR + k]]


def mirror_part(me, net, rows, own, buf):
    p1, s = me.p1, me.s
    pack, tab = buf.pack, own.table
    sum_far = own.sum_far
    mirror_products(rows, own, buf, sum_far)
    sib = []
    for q2 in (p1 + 2, p1 + 1, p1 + 3, p1):
        base = (q2 % SIDE) * SIDE
        for q1 in range(SIDE):
            pack[base + q1] = sum_far[tab[T_LAST_FAR + (1 - s) * 16 + base + q1]]
        sib.append(
            net.copy(pack.at[pl.ds(base, SIDE)], buf.sib.at[pl.ds(base, SIDE)], me.sib)
        )
    return sib


def reduce_steps(me, net, own, buf, sib, result):
    p1, p2, z, s = me.p1, me.p2, me.z, me.s
    total, nears, tab = buf.total, buf.nears, own.table
    sum_far = own.sum_far
    sum_near = own.sum_near
    zs = {}
    order1 = (p1 + 2, p1 + 1, p1 + 3, p1)

    def z_block(sign, d):
        return (z + d) % N_COL if sign == "p" else (z + N_COL - d) % N_COL

    def z_step(d, parts=(("p", 0), ("m", 0), ("p", 1), ("m", 1))):
        for sign, j in parts:
            way = 0 if sign == "p" else 1
            if (sign, d + 1, j) in zs:
                zs[sign, d + 1, j].wait_recv()
                nears[z_block(sign, d), piece(j)] += buf.zin[way, d, piece(j)]
            if d:
                zs[sign, d, j] = net.copy(
                    nears.at[z_block(sign, d), piece(j)],
                    buf.zin.at[way, d - 1, piece(j)],
                    (me.zp, me.zm)[way],
                )

    def at(q1, q2):
        return (q2 % SIDE) * SIDE + q1 % SIDE

    def whole(i, q2):
        sib[i].wait_recv()
        for q1 in range(SIDE):
            b = at(q1, q2)
            total[b] = sum_far[tab[T_LAST_FAR + s * 16 + b]] + buf.sib[b]

    whole(0, p2 + 2)
    r2 = (me.r2p, me.r2m)
    ahead = [
        net.copy(total.at[at(q1, p2 + 2)], buf.ring2a.at[i], r2[i % 2])
        for i, q1 in enumerate(order1)
    ]
    whole(1, p2 + 1)
    whole(2, p2 + 3)
    beside = (p2 + 1, p2 + 3)
    plain_copies = [
        net.copy(
            total.at[at(q1, beside[1 - i % 2])], buf.ring2b.at[1 - i % 2, i], r2[1 - i % 2]
        )
        for i, q1 in enumerate(order1)
    ]
    yield
    upper_products(own, buf, sum_near)
    for a in range(N_COL):
        nears[a] = sum_near[tab[T_LAST_NEAR + a]]
    z_step(4, (("p", 0), ("m", 1)))
    z_step(3, (("m", 0), ("p", 1)))
    yield
    summed_copies = []
    for i, q1 in enumerate(order1):
        ahead[i].wait_recv()
        b = at(q1, beside[i % 2])
        total[b] += buf.ring2a[i]
        summed_copies.append(net.copy(total.at[b], buf.ring2b.at[i % 2, i], r2[i % 2]))
        if i == 1:
            yield
    z_step(3, (("p", 0), ("m", 1)))
    whole(3, p2)
    yield
    z_step(2)
    yield
    col = buf.col

    def gathered(i):
        plain_copies[i].wait_recv()
        summed_copies[i].wait_recv()
        col[i] = total[at(order1[i], p2)] + (buf.ring2b[0, i] + buf.ring2b[1, i])

    gathered(0)
    on = net.copy(col.at[0], buf.ring1a.at[0], me.r1far)
    yield
    gathered(1)
    b1 = net.copy(col.at[1], buf.ring1b.at[0], me.r1p)
    yield
    z_step(1)
    yield
    gathered(2)
    b2 = net.copy(col.at[2], buf.ring1b.at[1], me.r1m)
    gathered(3)
    yield
    z_step(0)
    part = col[3] + nears[z]
    yield
    b1.wait_recv()
    b2.wait_recv()
    on.wait_recv()
    result[...] = part + (buf.ring1b[0] + buf.ring1b[1]) + buf.ring1a[0]


def pipe_steps(me, net, rows, own, bufs, grams, image):
    for it in range(ITERS):
        buf = bufs[it]
        buf.far[me.slot(me.p1, me.p2)] = image
        buf.near[me.z] = image
        sib = []

        def near_done():
            sib.extend(mirror_part(me, net, rows, own, buf))

        yield from gather_steps(me, net, buf, near_done)
        yield from reduce_steps(me, net, own, buf, sib, grams[it].image)
        image = grams[it].image[...]
        yield it


def gram_steps(me, net, own, buf, image):
    buf.gram[...] = exact(image, image, ((1,), (1,))) * (1.0 / NODES)
    gz, gx, gy, gsum = buf.gz, buf.gx, buf.gy, buf.gsum

    def rows(c):
        return pl.ds(pl.multiple_of((c % N_COL) * PART, PART), PART)

    ones = [
        net.copy(buf.gram.at[rows(me.z + d)], gz.at[d], me.z_peer(d)) for d in range(1, N_COL)
    ]
    yield
    for one in ones:
        one.wait_recv()
    part = buf.gram[rows(me.z), :]
    for d in range(1, N_COL):
        part = part + gz[d]
    here = me.x * 2 + me.s
    gx[here] = part
    ones = [net.copy(gx.at[here], gx.at[here], me.x_peer(*o)) for o in X_OFFSETS]
    yield
    for one in ones:
        one.wait_recv()
    part = gx[0]
    for i in range(1, N_COL):
        part = part + gx[i]
    gy[me.y] = part
    ones = [net.copy(gy.at[me.y], gy.at[me.y], me.y_peer(d)) for d in range(1, SIDE)]
    yield
    for one in ones:
        one.wait_recv()
    part = gy[0]
    for i in range(1, SIDE):
        part = part + gy[i]
    gsum[rows(me.z), :] = part
    ones = [
        net.copy(gsum.at[rows(me.z)], gsum.at[rows(me.z)], me.z_peer(d))
        for d in range(1, N_COL)
    ]
    yield
    for one in ones:
        one.wait_recv()
    yield
    yield from cholesky_steps(own, gsum)


def cholesky_steps(own, gsum):
    upper, inverse = own.upper, own.inverse
    lane = lax.broadcasted_iota(jnp.int32, (VEC, VEC), 1)
    sub = lax.broadcasted_iota(jnp.int32, (VEC, VEC), 0)
    upper[...] = gsum[...]
    inverse[...] = jnp.where(lane == sub, 1.0, 0.0).astype(F32)
    strip = sub[:PANEL]
    for o in range(0, VEC, PANEL):
        p = upper[o : o + PANEL, :]
        a = inverse[o : o + PANEL, :]
        for first in range(0, PANEL, GROUP):
            columns = [
                jnp.broadcast_to(p[:, o + j : o + j + 1], (PANEL, VEC))
                for j in range(first, first + GROUP)
            ]
            for t in range(GROUP):
                j = first + t
                if j == PANEL - 1:
                    continue
                c = columns[t]
                m = jnp.where(strip > j, c, 0.0) * (1.0 / c[j : j + 1])
                for w in range(t + 1, GROUP):
                    columns[w] = columns[w] - m * c[first + w : first + w + 1]
                p, a = p - m * p[j : j + 1], a - m * a[j : j + 1]
        pivots = jnp.sum(jnp.where(lane[:PANEL] == strip + o, p, 0.0), axis=1, keepdims=True)
        scale = 1.0 / jnp.sqrt(pivots)
        p, a = p * scale, a * scale
        upper[o : o + PANEL, :] = p
        inverse[o : o + PANEL, :] = a
        if o + PANEL < VEC:
            below = p.T[o + PANEL :]
            upper[o + PANEL :, :] -= exact(below, p, ((1,), (0,)))
            inverse[o + PANEL :, :] -= exact(below, a, ((1,), (0,)))
        yield


def prepare_steps(rows, cols, count, own, loading):
    tab = own.table
    live = count[0]

    def latest(keys, key, before):
        found = jnp.int32(0)
        for k in range(SLOTS):
            hit = (keys[k] == key) & (k < before)
            found = jnp.where(hit, k + 1, found)
        return found

    cols_at = [cols[0, k] for k in range(SLOTS)]
    rows_at = [rows[0, k] for k in range(SLOTS)]

    @pl.loop(0, SLOTS)
    def _(k):
        b = cols[0, k]
        s, x, y = b % 2, (b // 2) % SIDE, b // (2 * SIDE)
        tab[T_FAR + k] = s * 16 + jnp.where(s == 0, y * SIDE + x, x * SIDE + y)
        tab[T_PREV_FAR + k] = latest(cols_at, b, jnp.minimum(k, live))
        tab[T_PREV_NEAR + k] = latest(rows_at, rows[0, k], jnp.minimum(k, live))

    yield

    @pl.loop(0, N_ROW)
    def _(i):
        s, q2, q1 = i // 16, (i // SIDE) % SIDE, i % SIDE
        x, y = q1 * (1 - s) + q2 * s, q2 * (1 - s) + q1 * s
        tab[T_LAST_FAR + i] = latest(cols_at, y * 8 + x * 2 + s, live)

    @pl.loop(0, N_COL)
    def _(i):
        tab[T_LAST_NEAR + i] = latest(rows_at, i, live)

    yield
    loading.wait()
    for first in range(0, SLOTS, 6):

        @pl.loop(first, first + 6)
        def _(k):
            own.high[k], own.low[k] = split(own.tiles_in[k])

        yield


def kernel(names, rows, cols, count, start, tiles, basis, factor, *scratch):
    own_names, gram_names, block_names = names
    refs = iter(scratch)
    take = lambda keys: SimpleNamespace(**{key: next(refs) for key in keys})
    own = take(own_names)
    grams = [take(gram_names) for _ in range(ITERS)]
    bufs = [take(block_names) for _ in range(ITERS)]
    me = place()
    loading = pltpu.make_async_copy(tiles, own.tiles_in, own.tile_sem)
    loading.start()
    image = start[...].T
    for ref in (own.sum_far, own.sum_near):
        ref[0] = jnp.zeros((VEC, TILE), F32)
    enter(me)

    net = Net(own.send, own.recv)
    beside = prepare_steps(rows, cols, count, own, loading)
    tick, every = 0, 1
    for at in pipe_steps(me, net, rows, own, bufs, grams, image):
        if at == 0:
            beside = gram_steps(me, net, own, grams[0], grams[0].image[...])
            tick, every = 0, EVERY
        if tick % every == 0:
            next(beside, None)
        tick += 1
    for _ in beside:
        pass
    image = exact(own.inverse[...], grams[1].image[...], ((1,), (0,)))
    for _ in gram_steps(me, net, own, grams[1], image):
        pass
    basis[...] = exact(own.inverse[...], image, ((1,), (0,))).T
    lane = lax.broadcasted_iota(jnp.int32, (VEC, VEC), 1)
    sub = lax.broadcasted_iota(jnp.int32, (VEC, VEC), 0)
    factor[...] = jnp.where(lane >= sub, own.upper[...], 0.0).T
    net.drain()


def shards(start, tiles, tile_rows, tile_cols, tile_count):
    own, gram, block = own_scratch(), gram_scratch(), block_scratch()
    names = (tuple(own), tuple(gram), tuple(block))
    vmem = pl.BlockSpec(memory_space=pltpu.VMEM)
    smem = pl.BlockSpec(memory_space=pltpu.SMEM)

    def body(*refs):
        kernel(names, *refs)

    return pl.pallas_call(
        body,
        out_shape=(
            jax.ShapeDtypeStruct((TILE, VEC), F32),
            jax.ShapeDtypeStruct((VEC, VEC), F32),
        ),
        in_specs=[smem, smem, smem, vmem, pl.BlockSpec(memory_space=pl.ANY)],
        out_specs=(vmem, vmem),
        scratch_shapes=[
            *own.values(),
            *(ref for _ in range(ITERS) for ref in gram.values()),
            *(ref for _ in range(ITERS) for ref in block.values()),
        ],
        compiler_params=pltpu.CompilerParams(
            collective_id=0, has_side_effects=True, vmem_limit_bytes=62 * 1024 * 1024
        ),
    )(tile_rows, tile_cols, tile_count, start, tiles[0])


def solution(mesh):
    placed = (
        P(("row", "col"), None),
        P(("row", "col"), None, None, None),
        P(("row", "col"), None),
        P(("row", "col"), None),
        P(("row", "col")),
    )
    return jax.shard_map(
        shards,
        mesh=mesh,
        in_specs=placed,
        out_specs=(P(("row", "col"), None), P()),
        check_vma=False,
    )
```
